32 devices in a mesh: grp: 2 (over y), pre: 4 (over z), stg: 2 (over x), tp: 2 (over core).
Axes of the slice: x: 2, y: 2, z: 4, core: 2. Of those that a mesh axis runs over, the one named last changes fastest.
Arguments:
- queries: bfloat16 [32, 256, 4096], P(('grp', 'pre'), 'stg', 'tp'), parts along dimension 0, may hold values from -6 to 6
- doc_keys: bfloat16 [32, 256, 512], P(('grp', 'pre'), 'stg', 'tp'), parts along dimension 0, may hold values from -6 to 6
- doc_values: bfloat16 [32, 256, 512], P(('grp', 'pre'), 'stg', 'tp'), parts along dimension 0, may hold values from -48 to 48
- prefix_keys: bfloat16 [8, 1024, 512], P(('grp', 'pre'), None, 'tp'), parts along dimension 0, may hold values from -6 to 6
- prefix_values: bfloat16 [8, 1024, 512], P(('grp', 'pre'), None, 'tp'), parts along dimension 0, may hold values from -48 to 48
- template: int32 [32, 1], P(('grp', 'pre')), parts along dimension 0, may hold values from 0 to 3; in each aligned block of 4 rows (0 to 3, 4 to 7, ...) no two rows name the same one
- owner_table: int32 [8], P('grp'), parts along dimension 0, may hold values from 0 to 3, each once
Outputs:
- attended: bfloat16 [32, 256, 4096], P(('grp', 'pre'), 'stg', 'tp'), parts along dimension 0
The draws below stay inside these ranges and needn't reach their ends.
There are 2 independent parts, one for each index of `grp`. The reference program is written for one: setup_inputs(seed, part) draws one part's arguments, and reference() takes and returns one part's arrays. A program takes and returns all parts, laid end to end along the dimension named above; each array names one. Nothing has to cross between parts.
Inputs may be any that keep to these rules, and one draw needn't show every extreme that they name: No template is named by more than one of the 4 documents of one index of pre. `owner_table`: each owner holds the cache of exactly one template.
All inputs are finite; a program needn't handle non-finite values.
Results may differ from the reference program's by a relative error of at most 0.0034.
Values may be sent and summed in bfloat16 or wider, within the bound.
A program may use at most 128 MiB of HBM per device.

```python
import math
import jax
import jax.numpy as jnp
import numpy as np
from jax import lax

H = 32
KVH = 4
HD = 128
PREF = 1024
DOC_DEV = 4
DOCS = 16
SEQ = 256
NTEMP = 4


def draw_queries(key, part):
    drawn = jnp.clip(jax.random.normal(jax.random.fold_in(key, 11), (DOCS, SEQ, H, HD), jnp.float32), -5.5, 5.5)
    return drawn.reshape(DOCS, SEQ, H * HD).astype(jnp.bfloat16)


def draw_prefix_keys(key, part):
    drawn = jnp.clip(jax.random.normal(jax.random.fold_in(key, 21), (NTEMP, PREF, KVH, HD), jnp.float32), -5.5, 5.5)
    return drawn.reshape(NTEMP, PREF, KVH * HD).astype(jnp.bfloat16)


def draw_doc_keys(key, part):
    drawn = jnp.clip(2.5 * jax.random.normal(jax.random.fold_in(key, 31), (DOCS, SEQ, KVH, HD), jnp.float32), -6.0, 6.0)
    return drawn.reshape(DOCS, SEQ, KVH * HD).astype(jnp.bfloat16)


def steps_of(stream_key, extent, cuts, smallest, largest):
    gain = 1.0
    for dim, shards_of in cuts:
        steps = jax.random.uniform(jax.random.fold_in(jax.random.fold_in(stream_key, 6), dim), (shards_of,), jnp.float32, smallest / len(cuts), largest / len(cuts))
        gain = gain * jnp.repeat(jnp.exp(steps), extent[dim] // shards_of).reshape((-1,) + (1,) * (len(extent) - 1 - dim))
    return gain


def assign_block(stream_key, own, number, rows, count, top, limit, skew):
    sequence = jax.random.permutation(stream_key, count)
    crowded, ordinary = load_shares(count, rows * top, limit, skew, True), load_shares(count, rows * top, limit, skew, False)
    places = jnp.arange(count)

    def named(tallies, rotation):
        used = int((tallies > 0).sum())
        fixed = max(1, used // 4)
        moved = fixed + (places - fixed + rotation * (used - fixed)) % max(1, count - fixed)
        return jnp.zeros((count,), jnp.int32).at[sequence[jnp.where(places < fixed, places, moved)]].set(jnp.asarray(tallies, jnp.int32))

    tallies = jnp.where(number % 4 == 0, named(crowded, number // 4), named(ordinary, number - number // 4 - 1))
    mixed = jax.random.permutation(jax.random.fold_in(own, 3), count)
    giver, taker = mixed[0:count // 2 * 2:2], mixed[1:count // 2 * 2:2]
    slack = jnp.minimum(tallies[giver] - 1, limit - tallies[taker]) // 2
    slack = jnp.where((giver == sequence[0]) | (taker == sequence[0]) | (tallies[taker] == 0), 0, jnp.maximum(slack, 0))
    moved = jax.random.randint(jax.random.fold_in(own, 4), (count // 2,), 0, 1 << 20) % (slack + 1)
    tallies = tallies.at[giver].add(-moved).at[taker].add(moved)
    members = jnp.searchsorted(jnp.cumsum(tallies), jnp.arange(rows * top), side="right").astype(jnp.int32)
    listing = members.reshape(top, rows).T
    listing = listing[jax.random.permutation(jax.random.fold_in(own, 1), rows)]
    rotation = jax.random.randint(jax.random.fold_in(own, 2), (rows, 1), 0, top)
    return jnp.take_along_axis(listing, (jnp.arange(top)[None, :] + rotation) % top, axis=1)


def load_shares(amount, total, limit, slope, full):
    portions = [(1 << 20) // math.isqrt(standing ** slope) + 1 for standing in range(1, amount + 1)]
    largest = limit if full else min(limit, max(-(-total // amount), total * portions[0] // sum(portions)))
    least = 1 if total - largest >= amount - 1 else 0
    holding, rest = [largest] + [least] * (amount - 1), total - largest - least * (amount - 1)
    while rest > 0:
        movable = [i for i in range(1, amount) if holding[i] < largest] or [i for i in range(1, amount) if holding[i] < limit]
        mass, remaining = sum([portions[i] for i in movable]), rest
        for i in movable:
            addition = min(limit - holding[i], max(1, remaining * portions[i] // mass), rest)
            holding[i] = holding[i] + addition
            rest = rest - addition
    return np.array(holding)


def gaussian(key, shape, spread, bound, shards=(), held_as=jnp.bfloat16):
    values = spread * jax.random.normal(key, shape, jnp.float32)
    if shards:
        values = values * steps_of(key, shape, shards, -0.22, 0.18)
    return jnp.clip(values, -bound, bound).astype(held_as)


def setup_inputs(seed: int = 0, part: int = 0) -> dict:
    splits = jax.random.split(jax.random.key(seed), 8)
    part_splits = jax.random.split(jax.random.fold_in(splits[7], part), 8)
    queries = draw_queries(jax.random.fold_in(jax.random.fold_in(splits[7], part), 71), part)
    doc_keys = draw_doc_keys(jax.random.fold_in(jax.random.fold_in(splits[7], part), 71), part)
    doc_values = gaussian(part_splits[2], (DOCS, SEQ, KVH * HD), 8.0, 48.0, ((0, 4), (1, 2), (2, 2)))
    prefix_keys = draw_prefix_keys(jax.random.fold_in(jax.random.fold_in(splits[7], part), 71), part)
    prefix_values = gaussian(part_splits[4], (NTEMP, PREF, KVH * HD), 8.0, 48.0, ((0, 4), (2, 2)))
    template_keys = jax.random.split(jax.random.fold_in(part_splits[5], 1), DOCS // DOC_DEV)
    template_turns = jax.random.permutation(jax.random.fold_in(part_splits[5], 3), DOCS // DOC_DEV)
    template = jax.vmap(lambda own, number: assign_block(jax.random.fold_in(part_splits[5], 2), own, number, DOC_DEV, NTEMP, 1, 1, 2))(template_keys, template_turns).reshape((DOCS, 1))
    owner_table = jax.random.permutation(part_splits[6], NTEMP).astype(jnp.int32)
    return {"queries": queries, "doc_keys": doc_keys, "doc_values": doc_values, "prefix_keys": prefix_keys, "prefix_values": prefix_values, "template": template, "owner_table": owner_table}


def attend(queries, keys_in, values_in, visible):
    row_count = queries.shape[0]
    length = keys_in.shape[0]
    groups = H // KVH
    query_heads = queries.astype(jnp.float32).reshape(row_count, KVH, groups, HD)
    key_heads = keys_in.astype(jnp.float32).reshape(length, KVH, HD)
    value_heads = values_in.astype(jnp.float32).reshape(length, KVH, HD)
    scores = jnp.einsum("tkgh,skh->kgts", query_heads, key_heads) * (HD ** -0.5)
    scores = jnp.where(visible, scores, -1e30)
    highest = jnp.max(scores, axis=-1, keepdims=True)
    weights = jnp.where(visible, jnp.exp(scores - highest), 0.0)
    totals = jnp.sum(weights, axis=-1)
    rounded = lax.optimization_barrier(weights.astype(jnp.bfloat16)).astype(jnp.float32)
    summed = jnp.einsum("kgts,skh->tkgh", rounded, value_heads)
    output = summed / jnp.transpose(totals, (2, 0, 1))[..., None]
    log_total = jnp.transpose(highest[..., 0] + jnp.log(totals), (2, 0, 1))
    return output, log_total


def reference(queries, doc_keys, doc_values, prefix_keys, prefix_values, template, owner_table):
    holders = owner_table[template[:, 0]].astype(jnp.int32)
    positions = jnp.arange(SEQ, dtype=jnp.int32)
    causal = positions[:, None] >= positions[None, :]
    everything = jnp.ones((SEQ, PREF), dtype=jnp.bool_)

    def score_one(packed):
        doc_query, doc_key, doc_value, holder = packed
        cache_keys = lax.dynamic_index_in_dim(prefix_keys, holder, 0, keepdims=False)
        cache_values = lax.dynamic_index_in_dim(prefix_values, holder, 0, keepdims=False)
        prefix_out, prefix_log = attend(doc_query, cache_keys, cache_values, everything)
        prefix_out = lax.optimization_barrier(prefix_out.astype(jnp.bfloat16)).astype(jnp.float32)
        local_out, local_log = attend(doc_query, doc_key, doc_value, causal)
        joint_log = jnp.logaddexp(prefix_log, local_log)
        mixture = jnp.exp(prefix_log - joint_log)[..., None] * prefix_out + jnp.exp(local_log - joint_log)[..., None] * local_out
        return mixture.reshape(SEQ, H * HD).astype(jnp.bfloat16)

    return lax.map(score_one, (queries, doc_keys, doc_values, holders))
```

```python
import functools
import math

import jax
import jax.numpy as jnp
from jax import lax
from jax.experimental import pallas as pl
from jax.experimental.pallas import tpu as pltpu
from jax.sharding import PartitionSpec as P

H = 32
KVH = 4
HD = 128


def prefix_part(rows_in, cache_keys, cache_values, kv_local):
    row_count = rows_in.shape[0]
    groups = H // KVH
    length = cache_keys.shape[0]
    query_heads = rows_in.reshape(row_count, kv_local, groups, HD)
    key_heads = cache_keys.reshape(length, kv_local, HD)
    value_heads = cache_values.reshape(length, kv_local, HD)
    scores = jnp.einsum(
        "tkgh,skh->kgts", query_heads, key_heads, preferred_element_type=jnp.float32
    ) * HD ** (-0.5)
    highest = jnp.max(scores, axis=-1, keepdims=True)
    weights = jnp.exp(scores - highest)
    totals = jnp.sum(weights, axis=-1)
    summed = jnp.einsum(
        "kgts,skh->tkgh",
        weights.astype(jnp.bfloat16),
        value_heads,
        preferred_element_type=jnp.float32,
    )
    output = summed / jnp.transpose(totals, (2, 0, 1))[..., None]
    log_total = jnp.transpose(highest[..., 0] + jnp.log(totals), (2, 0, 1))
    return (
        output.reshape(row_count, kv_local * groups * HD).astype(jnp.bfloat16),
        log_total.reshape(row_count, kv_local * groups),
    )


def shards(queries, doc_keys, doc_values, prefix_keys, prefix_values, template, owner_table):
    kv_local = KVH // lax.axis_size("tp")
    groups = H // KVH
    docs_here, span_len, features = queries.shape
    templates_all = owner_table.shape[0]
    matches = template == jnp.arange(templates_all, dtype=jnp.int32)[None, :]
    holders = jnp.sum(jnp.where(matches, owner_table[None, :], 0), axis=1)
    whole_keys, whole_values = (
        lax.all_gather(prefix_keys, "pre", axis=0, tiled=True),
        lax.all_gather(prefix_values, "pre", axis=0, tiled=True),
    )

    def per_document(packed):
        doc_rows, holder = packed
        cache_keys = lax.dynamic_index_in_dim(whole_keys, holder, 0, keepdims=False)
        cache_values = lax.dynamic_index_in_dim(whole_values, holder, 0, keepdims=False)
        return prefix_part(doc_rows, cache_keys, cache_values, kv_local)

    prefix_rounded, prefix_log = lax.map(per_document, (queries, holders))
    prefix_out = prefix_rounded.astype(jnp.float32)
    query_heads = queries.reshape(docs_here, span_len, kv_local, groups, HD)
    query_pos = lax.axis_index("stg") * span_len + jnp.arange(span_len, dtype=jnp.int32)
    running_max = jnp.full((docs_here, kv_local, groups, span_len), -1e30, jnp.float32)
    key_piece = lax.all_gather(doc_keys, "stg", axis=1, tiled=True)
    value_piece = lax.all_gather(doc_values, "stg", axis=1, tiled=True)
    piece_len = key_piece.shape[1]
    key_heads = key_piece.reshape(docs_here, piece_len, kv_local, HD)
    value_heads = value_piece.reshape(docs_here, piece_len, kv_local, HD)
    scores = jnp.einsum(
        "dtkgh,dskh->dkgts", query_heads, key_heads, preferred_element_type=jnp.float32
    ) * HD ** (-0.5)
    key_pos = jnp.arange(piece_len, dtype=jnp.int32)
    visible = query_pos[:, None] >= key_pos[None, :]
    scores = jnp.where(visible, scores, -1e30)
    new_max = jnp.maximum(running_max, jnp.max(scores, axis=-1))
    weights = jnp.where(visible, jnp.exp(scores - new_max[..., None]), 0.0)
    new_sum = jnp.sum(weights, axis=-1)
    added = jnp.einsum(
        "dkgts,dskh->dkgth",
        weights.astype(jnp.bfloat16),
        value_heads,
        preferred_element_type=jnp.float32,
    )
    local_heads = jnp.transpose(added / new_sum[..., None], (0, 3, 1, 2, 4))
    local_log = jnp.transpose(new_max + jnp.log(new_sum), (0, 3, 1, 2))
    prefix_heads = prefix_out.reshape(docs_here, span_len, kv_local, groups, HD)
    prefix_log = prefix_log.reshape(docs_here, span_len, kv_local, groups)
    joint_log = jnp.logaddexp(prefix_log, local_log)
    mixture = (
        jnp.exp(prefix_log - joint_log)[..., None] * prefix_heads
        + jnp.exp(local_log - joint_log)[..., None] * local_heads
    )
    return mixture.reshape(docs_here, span_len, features).astype(jnp.bfloat16)


ROW_CHUNKS = 4
HEADS_TILE = 4
MESH = pl.DeviceIdType.MESH
NT = (((1,), (1,)), ((), ()))


def pick(me, table, step):
    chosen = 0
    for place, row in enumerate(table):
        chosen = chosen + row[step] * (me == place).astype(jnp.int32)
    return chosen


def shared_kernel(
    n, kv, q_hbm, dk_hbm, dv_hbm, pk_hbm, pv_hbm, tmpl, table, out_hbm,
    qv, own, prev, cache, held, first, stat, load_sem, own_sem, loc_send, loc_recv,
    up_send, down_send, z_send, x_send, recv, out_sem,
):
    docs, span, feats = qv.shape
    length = cache.shape[2]
    groups = feats // (kv * HD)
    rows_chunk = length // ROW_CHUNKS
    me, mine = lax.axis_index("pre"), lax.axis_index("stg")
    other = 1 - mine
    scale = HD ** (-0.5) * math.log2(math.e)

    loads = [
        pltpu.make_async_copy(q_hbm, qv, load_sem.at[0]),
        pltpu.make_async_copy(dk_hbm, own.at[0], load_sem.at[1]),
        pltpu.make_async_copy(dv_hbm, own.at[1], load_sem.at[2]),
    ]
    for array, source in enumerate((pk_hbm, pv_hbm)):
        for head in range(kv):
            slot = array * kv + head
            loads.append(pltpu.make_async_copy(
                source.at[0, :, head * HD:(head + 1) * HD], cache.at[me, slot], own_sem.at[slot]))

    barrier = pltpu.get_barrier_semaphore()

    @pl.when(me > 0)
    def _():
        pl.semaphore_signal(barrier, inc=1, device_id={"pre": me - 1}, device_id_type=MESH)

    @pl.when(me < n - 1)
    def _():
        pl.semaphore_signal(barrier, inc=1, device_id={"pre": me + 1}, device_id_type=MESH)

    pl.semaphore_signal(barrier, inc=1, device_id={"stg": other}, device_id_type=MESH)
    for load in loads:
        load.start()
    pl.semaphore_wait(barrier, jnp.where((me > 0) & (me < n - 1), 3, 2))

    def local_send(array):
        return pltpu.make_async_remote_copy(
            (dk_hbm, dv_hbm)[array], prev.at[array], loc_send.at[array], loc_recv.at[array],
            device_id={"stg": 1}, device_id_type=MESH)

    def own_send(head, array, part, step):
        source = (pk_hbm, pv_hbm)[array]
        slot = array * kv + head
        rows = pl.ds(part * rows_chunk, rows_chunk)
        return pltpu.make_async_remote_copy(
            source.at[0, rows, head * HD:(head + 1) * HD], cache.at[me, slot, rows],
            (up_send if step > 0 else down_send).at[slot, part], recv.at[me, slot, part],
            device_id={"pre": me + step}, device_id_type=MESH)

    def own_sends(action):
        for head in range(kv):
            @pl.when(mine == head % 2)
            def _():
                for array in range(2):
                    for part in range(ROW_CHUNKS):
                        @pl.when(me < n - 1)
                        def _():
                            action(own_send(head, array, part, 1))

                        @pl.when(me > 0)
                        def _():
                            action(own_send(head, array, part, -1))

    own_sends(lambda copy: copy.start())

    @pl.when(mine == 0)
    def _():
        for array in range(2):
            local_send(array).start()
        prev[...] = jnp.zeros_like(prev)

    def passed(owner, slot, part, axis):
        rows = pl.ds(pl.multiple_of(part * rows_chunk, rows_chunk), rows_chunk)
        piece = cache.at[owner, slot, rows]
        if axis == "x":
            return pltpu.make_async_remote_copy(
                piece, piece, x_send.at[owner, slot, part], recv.at[owner, slot, part],
                device_id={"stg": other}, device_id_type=MESH)
        target = jnp.where(owner > me, me - 1, me + 1)
        return pltpu.make_async_remote_copy(
            piece, piece, z_send.at[owner, slot, part], recv.at[owner, slot, part],
            device_id={"pre": target}, device_id_type=MESH)

    def goes_on(owner):
        return jnp.where(owner > me, me > 0, me < n - 1)

    def forward(owner, index):
        array, part = index // ROW_CHUNKS, index % ROW_CHUNKS
        slot = array * kv + mine
        passed(owner, slot, part, "x").wait_recv()
        passed(owner, slot, part, "x").start()

        @pl.when(goes_on(owner))
        def _():
            passed(owner, slot, part, "z").start()

    def arrive(owner, slot):
        for part in range(ROW_CHUNKS):
            passed(owner, slot, part, "x").wait_recv()

    holders = [table[tmpl[doc, 0]] for doc in range(docs)]

    def doc_of(owner):
        doc = 0
        for place in range(docs):
            doc = jnp.where(holders[place] == owner, place, doc)
        return doc

    tiles = groups // HEADS_TILE
    tile_rows = HEADS_TILE * span

    def queries_of(doc, head, tile):
        start = pl.multiple_of((head * groups + tile * HEADS_TILE) * HD, HEADS_TILE * HD)
        block = qv[doc, :, pl.ds(start, HEADS_TILE * HD)]
        return jnp.concatenate([block[:, i * HD:(i + 1) * HD] for i in range(HEADS_TILE)], axis=0)

    def prefix(queries, owner, head):
        scores = lax.dot_general(queries, cache[owner, head], NT, preferred_element_type=jnp.float32)
        peak = jnp.max(scores, axis=-1, keepdims=True)
        weights = jnp.exp2((scores - peak) * scale)
        total = jnp.sum(weights, axis=-1, keepdims=True)
        summed = jnp.dot(weights.astype(jnp.bfloat16), cache[owner, kv + head], preferred_element_type=jnp.float32)
        return (summed / total).astype(jnp.bfloat16), peak, total

    def local(queries, doc, head):
        lanes = pl.ds(pl.multiple_of(head * HD, HD), HD)
        keys = jnp.concatenate([prev[0, doc, :, lanes], own[0, doc, :, lanes]], axis=0)
        values = jnp.concatenate([prev[1, doc, :, lanes], own[1, doc, :, lanes]], axis=0)
        scores = lax.dot_general(queries, keys, NT, preferred_element_type=jnp.float32)
        row = lax.broadcasted_iota(jnp.int32, scores.shape, 0) % span
        column = lax.broadcasted_iota(jnp.int32, scores.shape, 1)
        visible = (column - span <= row) & (column >= span * other)
        scores = jnp.where(visible, scores, -1e30)
        peak = jnp.max(scores, axis=-1, keepdims=True)
        weights = jnp.where(visible, jnp.exp2((scores - peak) * scale), 0.0)
        total = jnp.sum(weights, axis=-1, keepdims=True)
        summed = jnp.dot(weights.astype(jnp.bfloat16), values, preferred_element_type=jnp.float32)
        return summed, peak, total

    def join(owner, head, tile, before, after):
        out_p, peak_p, total_p = before
        sum_l, peak_l, total_l = after
        peak = jnp.maximum(peak_p, peak_l)
        part_p = jnp.exp2((peak_p - peak) * scale)
        part_l = jnp.exp2((peak_l - peak) * scale)
        share = total_p * part_p
        mixed = (share * out_p.astype(jnp.float32) + part_l * sum_l) / (share + total_l * part_l)
        mixed = mixed.astype(jnp.bfloat16)
        start = pl.multiple_of((head * groups + tile * HEADS_TILE) * HD, HEADS_TILE * HD)
        held[owner, :, pl.ds(start, HEADS_TILE * HD)] = jnp.concatenate(
            [mixed[i * span:(i + 1) * span] for i in range(HEADS_TILE)], axis=1)

    order = [sorted(range(n), key=lambda o: (abs(o - m), o)) for m in range(n)]
    owners = [pick(me, order, step) for step in range(n)]
    doc_list = [doc_of(owner) for owner in owners]
    per_tile = 2 * ROW_CHUNKS // (2 * tiles)

    for load in loads:
        load.wait()

    for step in range(n):
        owner, doc = owners[step], doc_list[step]
        for half in range(2):
            head = (mine + half) % 2
            if step > 0 and half == 1:
                arrive(owner, head)
                arrive(owner, kv + head)
            if step == 1 and half == 0:
                @pl.when(mine == 1)
                def _():
                    for array in range(2):
                        local_send(array).wait_recv()

            def run(tile, carry):
                if step < n - 1:
                    for extra in range(per_tile):
                        forward(owners[step + 1], (half * tiles + tile) * per_tile + extra)
                queries = queries_of(doc, head, tile)
                if step == 0:
                    out, peak, total = prefix(queries, owner, head)
                    first[head, tile] = out
                    stat[head, tile, 0] = jnp.broadcast_to(peak, out.shape)
                    stat[head, tile, 1] = jnp.broadcast_to(total, out.shape)
                    return carry
                join(owner, head, tile, prefix(queries, owner, head), local(queries, doc, head))
                if step == 1:
                    queries = queries_of(doc_list[0], head, tile)
                    peak = stat[head, tile, 0][:, 0:1]
                    total = stat[head, tile, 1][:, 0:1]
                    join(owners[0], head, tile, (first[head, tile], peak, total), local(queries, doc_list[0], head))
                return carry

            lax.fori_loop(0, tiles, run, 0)
        if step > 0:
            pltpu.make_async_copy(held.at[owner], out_hbm.at[owner], out_sem.at[owner]).start()
        if step == 1:
            pltpu.make_async_copy(held.at[owners[0]], out_hbm.at[owners[0]], out_sem.at[owners[0]]).start()

    own_sends(lambda copy: copy.wait_send())

    @pl.when(mine == 0)
    def _():
        for array in range(2):
            local_send(array).wait_send()

    for step in range(1, n):
        owner = owners[step]
        for array in range(2):
            slot = array * kv + mine
            for part in range(ROW_CHUNKS):
                passed(owner, slot, part, "x").wait_send()

                @pl.when(goes_on(owner))
                def _():
                    passed(owner, slot, part, "z").wait_send()
    for owner in owners:
        pltpu.make_async_copy(held.at[owner], out_hbm.at[owner], out_sem.at[owner]).wait()


def reorder_kernel(tmpl, table, in_ref, out_ref):
    out_ref[...] = in_ref[...]


def shared(n, queries, doc_keys, doc_values, prefix_keys, prefix_values, template, owner_table):
    kv = KVH // lax.axis_size("tp")
    docs, span, feats = queries.shape
    length = prefix_keys.shape[1]
    groups = H // KVH
    tiles, tile_rows = groups // HEADS_TILE, HEADS_TILE * span
    slots = 2 * kv
    anywhere = pl.BlockSpec(memory_space=pl.ANY)
    scalars = pl.BlockSpec(memory_space=pltpu.SMEM)
    dma = pltpu.SemaphoreType.DMA
    scores = docs * feats // HD * span * (length + 2 * span)
    by_owner = pl.pallas_call(
        functools.partial(shared_kernel, n, kv),
        out_shape=jax.ShapeDtypeStruct(queries.shape, queries.dtype),
        in_specs=[anywhere] * 5 + [scalars] * 2,
        out_specs=anywhere,
        scratch_shapes=[
            pltpu.VMEM(queries.shape, jnp.bfloat16),
            pltpu.VMEM((2,) + doc_keys.shape, jnp.bfloat16),
            pltpu.VMEM((2,) + doc_keys.shape, jnp.bfloat16),
            pltpu.VMEM((n, slots, length, HD), jnp.bfloat16),
            pltpu.VMEM(queries.shape, jnp.bfloat16),
            pltpu.VMEM((kv, tiles, tile_rows, HD), jnp.bfloat16),
            pltpu.VMEM((kv, tiles, 2, tile_rows, HD), jnp.float32),
            dma((3,)),
            dma((slots,)),
            dma((2,)),
            dma((2,)),
            dma((slots, ROW_CHUNKS)),
            dma((slots, ROW_CHUNKS)),
            dma((n, slots, ROW_CHUNKS)),
            dma((n, slots, ROW_CHUNKS)),
            dma((n, slots, ROW_CHUNKS)),
            dma((n,)),
        ],
        compiler_params=pltpu.CompilerParams(
            collective_id=0, has_side_effects=True, vmem_limit_bytes=48 * 2 ** 20),
        cost_estimate=pl.CostEstimate(
            flops=4 * HD * scores, bytes_accessed=8 * 2 ** 20, transcendentals=scores),
    )(queries, doc_keys, doc_values, prefix_keys, prefix_values, template, owner_table)
    return pl.pallas_call(
        reorder_kernel,
        out_shape=jax.ShapeDtypeStruct(queries.shape, queries.dtype),
        grid_spec=pltpu.PrefetchScalarGridSpec(
            num_scalar_prefetch=2,
            grid=(docs,),
            in_specs=[pl.BlockSpec((1, span, feats), lambda d, tmpl, table: (table[tmpl[d, 0]], 0, 0))],
            out_specs=pl.BlockSpec((1, span, feats), lambda d, tmpl, table: (d, 0, 0)),
        ),
    )(template, owner_table, by_owner)


def route(queries, doc_keys, doc_values, prefix_keys, prefix_values, template, owner_table):
    n = lax.axis_size("pre")
    fits = (
        n == queries.shape[0] == owner_table.shape[0]
        and lax.axis_size("stg") == 2
        and KVH // lax.axis_size("tp") == 2
    )
    step = functools.partial(shared, n) if fits else shards
    return step(queries, doc_keys, doc_values, prefix_keys, prefix_values, template, owner_table)


def solution(mesh):
    return jax.shard_map(
        route,
        mesh=mesh,
        in_specs=(
            P(("grp", "pre"), "stg", "tp"),
            P(("grp", "pre"), "stg", "tp"),
            P(("grp", "pre"), "stg", "tp"),
            P(("grp", "pre"), None, "tp"),
            P(("grp", "pre"), None, "tp"),
            P(("grp", "pre"), None),
            P("grp"),
        ),
        out_specs=P(("grp", "pre"), "stg", "tp"),
        check_vma=False,
    )
```

```python
import functools
import math

import jax
import jax.numpy as jnp
from jax import lax
from jax.experimental import pallas as pl
from jax.experimental.pallas import tpu as pltpu
from jax.sharding import PartitionSpec as P

H = 32
KVH = 4
HD = 128


def prefix_part(rows_in, cache_keys, cache_values, kv_local):
    row_count = rows_in.shape[0]
    groups = H // KVH
    length = cache_keys.shape[0]
    query_heads = rows_in.reshape(row_count, kv_local, groups, HD)
    key_heads = cache_keys.reshape(length, kv_local, HD)
    value_heads = cache_values.reshape(length, kv_local, HD)
    scores = jnp.einsum(
        "tkgh,skh->kgts", query_heads, key_heads, preferred_element_type=jnp.float32
    ) * HD ** (-0.5)
    highest = jnp.max(scores, axis=-1, keepdims=True)
    weights = jnp.exp(scores - highest)
    totals = jnp.sum(weights, axis=-1)
    summed = jnp.einsum(
        "kgts,skh->tkgh",
        weights.astype(jnp.bfloat16),
        value_heads,
        preferred_element_type=jnp.float32,
    )
    output = summed / jnp.transpose(totals, (2, 0, 1))[..., None]
    log_total = jnp.transpose(highest[..., 0] + jnp.log(totals), (2, 0, 1))
    return (
        output.reshape(row_count, kv_local * groups * HD).astype(jnp.bfloat16),
        log_total.reshape(row_count, kv_local * groups),
    )


def shards(queries, doc_keys, doc_values, prefix_keys, prefix_values, template, owner_table):
    kv_local = KVH // lax.axis_size("tp")
    groups = H // KVH
    docs_here, span_len, features = queries.shape
    templates_all = owner_table.shape[0]
    matches = template == jnp.arange(templates_all, dtype=jnp.int32)[None, :]
    holders = jnp.sum(jnp.where(matches, owner_table[None, :], 0), axis=1)
    whole_keys, whole_values = (
        lax.all_gather(prefix_keys, "pre", axis=0, tiled=True),
        lax.all_gather(prefix_values, "pre", axis=0, tiled=True),
    )

    def per_document(packed):
        doc_rows, holder = packed
        cache_keys = lax.dynamic_index_in_dim(whole_keys, holder, 0, keepdims=False)
        cache_values = lax.dynamic_index_in_dim(whole_values, holder, 0, keepdims=False)
        return prefix_part(doc_rows, cache_keys, cache_values, kv_local)

    prefix_rounded, prefix_log = lax.map(per_document, (queries, holders))
    prefix_out = prefix_rounded.astype(jnp.float32)
    query_heads = queries.reshape(docs_here, span_len, kv_local, groups, HD)
    query_pos = lax.axis_index("stg") * span_len + jnp.arange(span_len, dtype=jnp.int32)
    running_max = jnp.full((docs_here, kv_local, groups, span_len), -1e30, jnp.float32)
    key_piece = lax.all_gather(doc_keys, "stg", axis=1, tiled=True)
    value_piece = lax.all_gather(doc_values, "stg", axis=1, tiled=True)
    piece_len = key_piece.shape[1]
    key_heads = key_piece.reshape(docs_here, piece_len, kv_local, HD)
    value_heads = value_piece.reshape(docs_here, piece_len, kv_local, HD)
    scores = jnp.einsum(
        "dtkgh,dskh->dkgts", query_heads, key_heads, preferred_element_type=jnp.float32
    ) * HD ** (-0.5)
    key_pos = jnp.arange(piece_len, dtype=jnp.int32)
    visible = query_pos[:, None] >= key_pos[None, :]
    scores = jnp.where(visible, scores, -1e30)
    new_max = jnp.maximum(running_max, jnp.max(scores, axis=-1))
    weights = jnp.where(visible, jnp.exp(scores - new_max[..., None]), 0.0)
    new_sum = jnp.sum(weights, axis=-1)
    added = jnp.einsum(
        "dkgts,dskh->dkgth",
        weights.astype(jnp.bfloat16),
        value_heads,
        preferred_element_type=jnp.float32,
    )
    local_heads = jnp.transpose(added / new_sum[..., None], (0, 3, 1, 2, 4))
    local_log = jnp.transpose(new_max + jnp.log(new_sum), (0, 3, 1, 2))
    prefix_heads = prefix_out.reshape(docs_here, span_len, kv_local, groups, HD)
    prefix_log = prefix_log.reshape(docs_here, span_len, kv_local, groups)
    joint_log = jnp.logaddexp(prefix_log, local_log)
    mixture = (
        jnp.exp(prefix_log - joint_log)[..., None] * prefix_heads
        + jnp.exp(local_log - joint_log)[..., None] * local_heads
    )
    return mixture.reshape(docs_here, span_len, features).astype(jnp.bfloat16)


ROW_CHUNKS = 4
HEADS_TILE = 4
MOVED = True
MESH = pl.DeviceIdType.MESH
NT = (((1,), (1,)), ((), ()))


def pick(me, table, step):
    chosen = 0
    for place, row in enumerate(table):
        chosen = chosen + row[step] * (me == place).astype(jnp.int32)
    return chosen


def shared_kernel(
    n, kv, q_hbm, dk_hbm, dv_hbm, pk_hbm, pv_hbm, tmpl, table, out_ref,
    qv, own, prev, cache, held, first, stat, load_sem, own_sem, loc_send, loc_recv,
    up_send, down_send, z_send, x_send, recv,
):
    docs, span, feats = qv.shape
    length = cache.shape[2]
    groups = feats // (kv * HD)
    rows_chunk = length // ROW_CHUNKS
    me, mine = lax.axis_index("pre"), lax.axis_index("stg")
    other = 1 - mine
    scale = HD ** (-0.5) * math.log2(math.e)

    loads = [
        pltpu.make_async_copy(q_hbm, qv, load_sem.at[0]),
        pltpu.make_async_copy(dk_hbm, own.at[0], load_sem.at[1]),
        pltpu.make_async_copy(dv_hbm, own.at[1], load_sem.at[2]),
    ]
    for array, source in enumerate((pk_hbm, pv_hbm)):
        for head in range(kv):
            slot = array * kv + head
            loads.append(pltpu.make_async_copy(
                source.at[0, :, head * HD:(head + 1) * HD], cache.at[me, slot], own_sem.at[slot]))

    barrier = pltpu.get_barrier_semaphore()

    @pl.when(me > 0)
    def _():
        pl.semaphore_signal(barrier, inc=1, device_id={"pre": me - 1}, device_id_type=MESH)

    @pl.when(me < n - 1)
    def _():
        pl.semaphore_signal(barrier, inc=1, device_id={"pre": me + 1}, device_id_type=MESH)

    pl.semaphore_signal(barrier, inc=1, device_id={"stg": other}, device_id_type=MESH)
    for load in loads:
        load.start()
    pl.semaphore_wait(barrier, jnp.where((me > 0) & (me < n - 1), 3, 2))

    def local_send(array):
        return pltpu.make_async_remote_copy(
            (dk_hbm, dv_hbm)[array], prev.at[array], loc_send.at[array], loc_recv.at[array],
            device_id={"stg": 1}, device_id_type=MESH)

    def own_send(head, array, part, step):
        source = (pk_hbm, pv_hbm)[array]
        slot = array * kv + head
        rows = pl.ds(part * rows_chunk, rows_chunk)
        return pltpu.make_async_remote_copy(
            source.at[0, rows, head * HD:(head + 1) * HD], cache.at[me, slot, rows],
            (up_send if step > 0 else down_send).at[slot, part], recv.at[me, slot, part],
            device_id={"pre": me + step}, device_id_type=MESH)

    pieces = [(array, part) for array in range(2) for part in range(ROW_CHUNKS)]
    stay = pieces[:-1] if MOVED else pieces
    carried = {
        0: [(0,) + piece for piece in stay],
        1: [(0,) + piece for piece in pieces[len(stay):]] + [(1,) + piece for piece in pieces],
    }

    def own_sends(action):
        for place, listed in carried.items():
            @pl.when(mine == place)
            def _():
                for head, array, part in listed:
                    @pl.when(me < n - 1)
                    def _():
                        action(own_send(head, array, part, 1))

                    @pl.when(me > 0)
                    def _():
                        action(own_send(head, array, part, -1))

    @pl.when(mine == 0)
    def _():
        for array in range(2):
            local_send(array).start()

    own_sends(lambda copy: copy.start())

    @pl.when(mine == 0)
    def _():
        prev[...] = jnp.zeros_like(prev)

    def passed(owner, slot, part, axis):
        rows = pl.ds(pl.multiple_of(part * rows_chunk, rows_chunk), rows_chunk)
        piece = cache.at[owner, slot, rows]
        if axis == "x":
            return pltpu.make_async_remote_copy(
                piece, piece, x_send.at[owner, slot, part], recv.at[owner, slot, part],
                device_id={"stg": other}, device_id_type=MESH)
        target = jnp.where(owner > me, me - 1, me + 1)
        return pltpu.make_async_remote_copy(
            piece, piece, z_send.at[owner, slot, part], recv.at[owner, slot, part],
            device_id={"pre": target}, device_id_type=MESH)

    def goes_on(owner):
        return jnp.where(owner > me, me > 0, me < n - 1)

    def relay(owner, slot, part):
        passed(owner, slot, part, "x").wait_recv()
        passed(owner, slot, part, "x").start()

        @pl.when(goes_on(owner))
        def _():
            passed(owner, slot, part, "z").start()

    moved_slot, moved_part = kv, ROW_CHUNKS - 1

    def forward(owner, index):
        @pl.when(MOVED & (mine == 1) & (index == 0))
        def _():
            relay(owner, moved_slot, moved_part)

        @pl.when((mine == 1) | (index < len(stay)))
        def _():
            relay(owner, index // ROW_CHUNKS * kv + mine, index % ROW_CHUNKS)

    def arrive_moved(owner):
        @pl.when(MOVED & (mine == 0))
        def _():
            passed(owner, moved_slot, moved_part, "x").wait_recv()

    def arrive(owner):
        for array, part in stay:
            passed(owner, array * kv + other, part, "x").wait_recv()

        @pl.when(MOVED & (mine == 0))
        def _():
            passed(owner, kv + other, moved_part, "x").wait_recv()

    holders = [table[tmpl[doc, 0]] for doc in range(docs)]

    def doc_of(owner):
        doc = 0
        for place in range(docs):
            doc = jnp.where(holders[place] == owner, place, doc)
        return doc

    tiles = groups // HEADS_TILE
    tile_rows = HEADS_TILE * span

    def queries_of(doc, head, tile):
        start = pl.multiple_of((head * groups + tile * HEADS_TILE) * HD, HEADS_TILE * HD)
        block = qv[doc, :, pl.ds(start, HEADS_TILE * HD)]
        return jnp.concatenate([block[:, i * HD:(i + 1) * HD] for i in range(HEADS_TILE)], axis=0)

    def prefix(queries, owner, head):
        scores = lax.dot_general(queries, cache[owner, head], NT, preferred_element_type=jnp.float32)
        peak = jnp.max(scores, axis=-1, keepdims=True)
        weights = jnp.exp2((scores - peak) * scale)
        total = jnp.sum(weights, axis=-1, keepdims=True)
        summed = jnp.dot(weights.astype(jnp.bfloat16), cache[owner, kv + head], preferred_element_type=jnp.float32)
        return (summed / total).astype(jnp.bfloat16), peak, total

    def local(queries, doc, head):
        lanes = pl.ds(pl.multiple_of(head * HD, HD), HD)
        keys = jnp.concatenate([prev[0, doc, :, lanes], own[0, doc, :, lanes]], axis=0)
        values = jnp.concatenate([prev[1, doc, :, lanes], own[1, doc, :, lanes]], axis=0)
        scores = lax.dot_general(queries, keys, NT, preferred_element_type=jnp.float32)
        row = lax.broadcasted_iota(jnp.int32, scores.shape, 0) % span
        column = lax.broadcasted_iota(jnp.int32, scores.shape, 1)
        visible = (column - span <= row) & (column >= span * other)
        scores = jnp.where(visible, scores, -1e30)
        peak = jnp.max(scores, axis=-1, keepdims=True)
        weights = jnp.where(visible, jnp.exp2((scores - peak) * scale), 0.0)
        total = jnp.sum(weights, axis=-1, keepdims=True)
        summed = jnp.dot(weights.astype(jnp.bfloat16), values, preferred_element_type=jnp.float32)
        return summed, peak, total

    def join(owner, head, tile, before, after):
        out_p, peak_p, total_p = before
        sum_l, peak_l, total_l = after
        peak = jnp.maximum(peak_p, peak_l)
        part_p = jnp.exp2((peak_p - peak) * scale)
        part_l = jnp.exp2((peak_l - peak) * scale)
        share = total_p * part_p
        mixed = (share * out_p.astype(jnp.float32) + part_l * sum_l) / (share + total_l * part_l)
        mixed = mixed.astype(jnp.bfloat16)
        start = pl.multiple_of((head * groups + tile * HEADS_TILE) * HD, HEADS_TILE * HD)
        held[owner, :, pl.ds(start, HEADS_TILE * HD)] = jnp.concatenate(
            [mixed[i * span:(i + 1) * span] for i in range(HEADS_TILE)], axis=1)

    order = [sorted(range(n), key=lambda o: (abs(o - m), o)) for m in range(n)]
    owners = [pick(me, order, step) for step in range(n)]
    doc_list = [doc_of(owner) for owner in owners]
    per_tile = 2 * ROW_CHUNKS // (2 * tiles)

    for load in loads:
        load.wait()

    for step in range(n):
        owner, doc = owners[step], doc_list[step]
        for half in range(2):
            head = (mine + half) % 2
            if step > 0:
                (arrive if half else arrive_moved)(owner)
            if step == 1 and half == 0:
                @pl.when(mine == 1)
                def _():
                    for array in range(2):
                        local_send(array).wait_recv()

            def run(tile, carry):
                if step < n - 1:
                    for extra in range(per_tile):
                        index = (half * tiles + tile) * per_tile + extra
                        for behind in (-step - 1, step + 1):
                            @pl.when((me + behind >= 0) & (me + behind < n))
                            def _():
                                forward(me + behind, index)
                queries = queries_of(doc, head, tile)
                if step == 0:
                    out, peak, total = prefix(queries, owner, head)
                    first[head, tile] = out
                    stat[head, tile, 0] = jnp.broadcast_to(peak, out.shape)
                    stat[head, tile, 1] = jnp.broadcast_to(total, out.shape)
                    return carry
                join(owner, head, tile, prefix(queries, owner, head), local(queries, doc, head))
                if step == 1:
                    queries = queries_of(doc_list[0], head, tile)
                    peak = stat[head, tile, 0][:, 0:1]
                    total = stat[head, tile, 1][:, 0:1]
                    join(owners[0], head, tile, (first[head, tile], peak, total), local(queries, doc_list[0], head))
                return carry

            lax.fori_loop(0, tiles, run, 0)

    for doc in range(docs):
        out_ref[doc] = held[holders[doc]]

    own_sends(lambda copy: copy.wait_send())

    @pl.when(mine == 0)
    def _():
        for array in range(2):
            local_send(array).wait_send()

    for step in range(1, n):
        owner = owners[step]
        for place, listed in carried.items():
            @pl.when(mine == place)
            def _():
                for head, array, part in listed:
                    slot = array * kv + head
                    passed(owner, slot, part, "x").wait_send()

                    @pl.when(goes_on(owner))
                    def _():
                        passed(owner, slot, part, "z").wait_send()


def shared(n, queries, doc_keys, doc_values, prefix_keys, prefix_values, template, owner_table):
    kv = KVH // lax.axis_size("tp")
    docs, span, feats = queries.shape
    length = prefix_keys.shape[1]
    groups = H // KVH
    tiles, tile_rows = groups // HEADS_TILE, HEADS_TILE * span
    slots = 2 * kv
    in_hbm = pl.BlockSpec(memory_space=pltpu.HBM)
    scalars = pl.BlockSpec(memory_space=pltpu.SMEM)
    dma = pltpu.SemaphoreType.DMA
    scores = docs * feats // HD * span * (length + 2 * span)
    return pl.pallas_call(
        functools.partial(shared_kernel, n, kv),
        out_shape=jax.ShapeDtypeStruct(queries.shape, queries.dtype),
        in_specs=[in_hbm] * 5 + [scalars] * 2,
        out_specs=pl.BlockSpec(memory_space=pltpu.VMEM),
        scratch_shapes=[
            pltpu.VMEM(queries.shape, jnp.bfloat16),
            pltpu.VMEM((2,) + doc_keys.shape, jnp.bfloat16),
            pltpu.VMEM((2,) + doc_keys.shape, jnp.bfloat16),
            pltpu.VMEM((n, slots, length, HD), jnp.bfloat16),
            pltpu.VMEM(queries.shape, jnp.bfloat16),
            pltpu.VMEM((kv, tiles, tile_rows, HD), jnp.bfloat16),
            pltpu.VMEM((kv, tiles, 2, tile_rows, HD), jnp.float32),
            dma((3,)),
            dma((slots,)),
            dma((2,)),
            dma((2,)),
            dma((slots, ROW_CHUNKS)),
            dma((slots, ROW_CHUNKS)),
            dma((n, slots, ROW_CHUNKS)),
            dma((n, slots, ROW_CHUNKS)),
            dma((n, slots, ROW_CHUNKS)),
        ],
        compiler_params=pltpu.CompilerParams(
            collective_id=0, has_side_effects=True, vmem_limit_bytes=62 * 2 ** 20),
        cost_estimate=pl.CostEstimate(
            flops=4 * HD * scores, bytes_accessed=8 * 2 ** 20, transcendentals=scores),
    )(queries, doc_keys, doc_values, prefix_keys, prefix_values, template, owner_table)


def route(queries, doc_keys, doc_values, prefix_keys, prefix_values, template, owner_table):
    n = lax.axis_size("pre")
    fits = (
        n == queries.shape[0] == owner_table.shape[0]
        and lax.axis_size("stg") == 2
        and KVH // lax.axis_size("tp") == 2
    )
    step = functools.partial(shared, n) if fits else shards
    return step(queries, doc_keys, doc_values, prefix_keys, prefix_values, template, owner_table)


def solution(mesh):
    return jax.shard_map(
        route,
        mesh=mesh,
        in_specs=(
            P(("grp", "pre"), "stg", "tp"),
            P(("grp", "pre"), "stg", "tp"),
            P(("grp", "pre"), "stg", "tp"),
            P(("grp", "pre"), None, "tp"),
            P(("grp", "pre"), None, "tp"),
            P(("grp", "pre"), None),
            P("grp"),
        ),
        out_specs=P(("grp", "pre"), "stg", "tp"),
        check_vma=False,
    )
```

```python
import functools
import math

import jax
import jax.numpy as jnp
from jax import lax
from jax.experimental import pallas as pl
from jax.experimental.pallas import tpu as pltpu
from jax.sharding import PartitionSpec as P

H = 32
KVH = 4
HD = 128


def prefix_part(rows_in, cache_keys, cache_values, kv_local):
    row_count = rows_in.shape[0]
    groups = H // KVH
    length = cache_keys.shape[0]
    query_heads = rows_in.reshape(row_count, kv_local, groups, HD)
    key_heads = cache_keys.reshape(length, kv_local, HD)
    value_heads = cache_values.reshape(length, kv_local, HD)
    scores = jnp.einsum(
        "tkgh,skh->kgts", query_heads, key_heads, preferred_element_type=jnp.float32
    ) * HD ** (-0.5)
    highest = jnp.max(scores, axis=-1, keepdims=True)
    weights = jnp.exp(scores - highest)
    totals = jnp.sum(weights, axis=-1)
    summed = jnp.einsum(
        "kgts,skh->tkgh",
        weights.astype(jnp.bfloat16),
        value_heads,
        preferred_element_type=jnp.float32,
    )
    output = summed / jnp.transpose(totals, (2, 0, 1))[..., None]
    log_total = jnp.transpose(highest[..., 0] + jnp.log(totals), (2, 0, 1))
    return (
        output.reshape(row_count, kv_local * groups * HD).astype(jnp.bfloat16),
        log_total.reshape(row_count, kv_local * groups),
    )


def shards(queries, doc_keys, doc_values, prefix_keys, prefix_values, template, owner_table):
    kv_local = KVH // lax.axis_size("tp")
    groups = H // KVH
    docs_here, span_len, features = queries.shape
    templates_all = owner_table.shape[0]
    matches = template == jnp.arange(templates_all, dtype=jnp.int32)[None, :]
    holders = jnp.sum(jnp.where(matches, owner_table[None, :], 0), axis=1)
    whole_keys, whole_values = (
        lax.all_gather(prefix_keys, "pre", axis=0, tiled=True),
        lax.all_gather(prefix_values, "pre", axis=0, tiled=True),
    )

    def per_document(packed):
        doc_rows, holder = packed
        cache_keys = lax.dynamic_index_in_dim(whole_keys, holder, 0, keepdims=False)
        cache_values = lax.dynamic_index_in_dim(whole_values, holder, 0, keepdims=False)
        return prefix_part(doc_rows, cache_keys, cache_values, kv_local)

    prefix_rounded, prefix_log = lax.map(per_document, (queries, holders))
    prefix_out = prefix_rounded.astype(jnp.float32)
    query_heads = queries.reshape(docs_here, span_len, kv_local, groups, HD)
    query_pos = lax.axis_index("stg") * span_len + jnp.arange(span_len, dtype=jnp.int32)
    running_max = jnp.full((docs_here, kv_local, groups, span_len), -1e30, jnp.float32)
    key_piece = lax.all_gather(doc_keys, "stg", axis=1, tiled=True)
    value_piece = lax.all_gather(doc_values, "stg", axis=1, tiled=True)
    piece_len = key_piece.shape[1]
    key_heads = key_piece.reshape(docs_here, piece_len, kv_local, HD)
    value_heads = value_piece.reshape(docs_here, piece_len, kv_local, HD)
    scores = jnp.einsum(
        "dtkgh,dskh->dkgts", query_heads, key_heads, preferred_element_type=jnp.float32
    ) * HD ** (-0.5)
    key_pos = jnp.arange(piece_len, dtype=jnp.int32)
    visible = query_pos[:, None] >= key_pos[None, :]
    scores = jnp.where(visible, scores, -1e30)
    new_max = jnp.maximum(running_max, jnp.max(scores, axis=-1))
    weights = jnp.where(visible, jnp.exp(scores - new_max[..., None]), 0.0)
    new_sum = jnp.sum(weights, axis=-1)
    added = jnp.einsum(
        "dkgts,dskh->dkgth",
        weights.astype(jnp.bfloat16),
        value_heads,
        preferred_element_type=jnp.float32,
    )
    local_heads = jnp.transpose(added / new_sum[..., None], (0, 3, 1, 2, 4))
    local_log = jnp.transpose(new_max + jnp.log(new_sum), (0, 3, 1, 2))
    prefix_heads = prefix_out.reshape(docs_here, span_len, kv_local, groups, HD)
    prefix_log = prefix_log.reshape(docs_here, span_len, kv_local, groups)
    joint_log = jnp.logaddexp(prefix_log, local_log)
    mixture = (
        jnp.exp(prefix_log - joint_log)[..., None] * prefix_heads
        + jnp.exp(local_log - joint_log)[..., None] * local_heads
    )
    return mixture.reshape(docs_here, span_len, features).astype(jnp.bfloat16)


ROW_CHUNKS = 4
HEADS_TILE = 4
MOVED = True
MESH = pl.DeviceIdType.MESH
NT = (((1,), (1,)), ((), ()))


def pick(me, table, step):
    chosen = 0
    for place, row in enumerate(table):
        chosen = chosen + row[step] * (me == place).astype(jnp.int32)
    return chosen


def shared_kernel(
    n, kv, q_hbm, dk_hbm, dv_hbm, pk_hbm, pv_hbm, tmpl, table, out_hbm,
    qv, own, prev, cache, held, first, stat, load_sem, own_sem, loc_send, loc_recv,
    up_send, down_send, z_send, x_send, recv, out_sem,
):
    docs, span, feats = qv.shape
    length = cache.shape[2]
    groups = feats // (kv * HD)
    rows_chunk = length // ROW_CHUNKS
    me, mine = lax.axis_index("pre"), lax.axis_index("stg")
    other = 1 - mine
    scale = HD ** (-0.5) * math.log2(math.e)

    loads = [
        pltpu.make_async_copy(q_hbm, qv, load_sem.at[0]),
        pltpu.make_async_copy(dk_hbm, own.at[0], load_sem.at[1]),
        pltpu.make_async_copy(dv_hbm, own.at[1], load_sem.at[2]),
    ]
    for array, source in enumerate((pk_hbm, pv_hbm)):
        for head in range(kv):
            slot = array * kv + head
            loads.append(pltpu.make_async_copy(
                source.at[0, :, head * HD:(head + 1) * HD], cache.at[me, slot], own_sem.at[slot]))

    barrier = pltpu.get_barrier_semaphore()

    @pl.when(me > 0)
    def _():
        pl.semaphore_signal(barrier, inc=1, device_id={"pre": me - 1}, device_id_type=MESH)

    @pl.when(me < n - 1)
    def _():
        pl.semaphore_signal(barrier, inc=1, device_id={"pre": me + 1}, device_id_type=MESH)

    pl.semaphore_signal(barrier, inc=1, device_id={"stg": other}, device_id_type=MESH)
    for load in loads:
        load.start()
    pl.semaphore_wait(barrier, jnp.where((me > 0) & (me < n - 1), 3, 2))

    def local_send(array):
        return pltpu.make_async_remote_copy(
            (dk_hbm, dv_hbm)[array], prev.at[array], loc_send.at[array], loc_recv.at[array],
            device_id={"stg": 1}, device_id_type=MESH)

    def own_send(head, array, part, step):
        source = (pk_hbm, pv_hbm)[array]
        slot = array * kv + head
        rows = pl.ds(part * rows_chunk, rows_chunk)
        return pltpu.make_async_remote_copy(
            source.at[0, rows, head * HD:(head + 1) * HD], cache.at[me, slot, rows],
            (up_send if step > 0 else down_send).at[slot, part], recv.at[me, slot, part],
            device_id={"pre": me + step}, device_id_type=MESH)

    pieces = [(array, part) for array in range(2) for part in range(ROW_CHUNKS)]
    stay = pieces[:-1] if MOVED else pieces
    carried = {
        0: [(0,) + piece for piece in stay],
        1: [(0,) + piece for piece in pieces[len(stay):]] + [(1,) + piece for piece in pieces],
    }

    def own_sends(action):
        for place, listed in carried.items():
            @pl.when(mine == place)
            def _():
                for head, array, part in listed:
                    @pl.when(me < n - 1)
                    def _():
                        action(own_send(head, array, part, 1))

                    @pl.when(me > 0)
                    def _():
                        action(own_send(head, array, part, -1))

    @pl.when(mine == 0)
    def _():
        for array in range(2):
            local_send(array).start()

    own_sends(lambda copy: copy.start())

    @pl.when(mine == 0)
    def _():
        prev[...] = jnp.zeros_like(prev)

    def passed(owner, slot, part, axis):
        rows = pl.ds(pl.multiple_of(part * rows_chunk, rows_chunk), rows_chunk)
        piece = cache.at[owner, slot, rows]
        if axis == "x":
            return pltpu.make_async_remote_copy(
                piece, piece, x_send.at[owner, slot, part], recv.at[owner, slot, part],
                device_id={"stg": other}, device_id_type=MESH)
        target = jnp.where(owner > me, me - 1, me + 1)
        return pltpu.make_async_remote_copy(
            piece, piece, z_send.at[owner, slot, part], recv.at[owner, slot, part],
            device_id={"pre": target}, device_id_type=MESH)

    def goes_on(owner):
        return jnp.where(owner > me, me > 0, me < n - 1)

    def relay(owner, slot, part):
        passed(owner, slot, part, "x").wait_recv()
        passed(owner, slot, part, "x").start()

        @pl.when(goes_on(owner))
        def _():
            passed(owner, slot, part, "z").start()

    moved_slot, moved_part = kv, ROW_CHUNKS - 1

    def forward(owner, index):
        @pl.when(MOVED & (mine == 1) & (index == 0))
        def _():
            relay(owner, moved_slot, moved_part)

        @pl.when((mine == 1) | (index < len(stay)))
        def _():
            relay(owner, index // ROW_CHUNKS * kv + mine, index % ROW_CHUNKS)

    def arrive_moved(owner):
        @pl.when(MOVED & (mine == 0))
        def _():
            passed(owner, moved_slot, moved_part, "x").wait_recv()

    def arrive(owner):
        for array, part in stay:
            passed(owner, array * kv + other, part, "x").wait_recv()

        @pl.when(MOVED & (mine == 0))
        def _():
            passed(owner, kv + other, moved_part, "x").wait_recv()

    holders = [table[tmpl[doc, 0]] for doc in range(docs)]

    def doc_of(owner):
        doc = 0
        for place in range(docs):
            doc = jnp.where(holders[place] == owner, place, doc)
        return doc

    tiles = groups // HEADS_TILE
    tile_rows = HEADS_TILE * span

    def queries_of(doc, head, tile):
        start = pl.multiple_of((head * groups + tile * HEADS_TILE) * HD, HEADS_TILE * HD)
        block = qv[doc, :, pl.ds(start, HEADS_TILE * HD)]
        return jnp.concatenate([block[:, i * HD:(i + 1) * HD] for i in range(HEADS_TILE)], axis=0)

    def prefix(queries, owner, head):
        scores = lax.dot_general(queries, cache[owner, head], NT, preferred_element_type=jnp.float32)
        peak = jnp.max(scores, axis=-1, keepdims=True)
        weights = jnp.exp2((scores - peak) * scale)
        total = jnp.sum(weights, axis=-1, keepdims=True)
        summed = jnp.dot(weights.astype(jnp.bfloat16), cache[owner, kv + head], preferred_element_type=jnp.float32)
        return (summed / total).astype(jnp.bfloat16), peak, total

    def local(queries, doc, head):
        lanes = pl.ds(pl.multiple_of(head * HD, HD), HD)
        keys = jnp.concatenate([prev[0, doc, :, lanes], own[0, doc, :, lanes]], axis=0)
        values = jnp.concatenate([prev[1, doc, :, lanes], own[1, doc, :, lanes]], axis=0)
        scores = lax.dot_general(queries, keys, NT, preferred_element_type=jnp.float32)
        row = lax.broadcasted_iota(jnp.int32, scores.shape, 0) % span
        column = lax.broadcasted_iota(jnp.int32, scores.shape, 1)
        visible = (column - span <= row) & (column >= span * other)
        scores = jnp.where(visible, scores, -1e30)
        peak = jnp.max(scores, axis=-1, keepdims=True)
        weights = jnp.where(visible, jnp.exp2((scores - peak) * scale), 0.0)
        total = jnp.sum(weights, axis=-1, keepdims=True)
        summed = jnp.dot(weights.astype(jnp.bfloat16), values, preferred_element_type=jnp.float32)
        return summed, peak, total

    def join(owner, head, tile, before, after):
        out_p, peak_p, total_p = before
        sum_l, peak_l, total_l = after
        peak = jnp.maximum(peak_p, peak_l)
        part_p = jnp.exp2((peak_p - peak) * scale)
        part_l = jnp.exp2((peak_l - peak) * scale)
        share = total_p * part_p
        mixed = (share * out_p.astype(jnp.float32) + part_l * sum_l) / (share + total_l * part_l)
        mixed = mixed.astype(jnp.bfloat16)
        start = pl.multiple_of((head * groups + tile * HEADS_TILE) * HD, HEADS_TILE * HD)
        held[owner, :, pl.ds(start, HEADS_TILE * HD)] = jnp.concatenate(
            [mixed[i * span:(i + 1) * span] for i in range(HEADS_TILE)], axis=1)

    order = [sorted(range(n), key=lambda o: (abs(o - m), o)) for m in range(n)]
    owners = [pick(me, order, step) for step in range(n)]
    doc_list = [doc_of(owner) for owner in owners]
    per_tile = 2 * ROW_CHUNKS // (2 * tiles)

    for load in loads:
        load.wait()

    for step in range(n):
        owner, doc = owners[step], doc_list[step]
        for half in range(2):
            head = (mine + half) % 2
            if step > 0:
                (arrive if half else arrive_moved)(owner)
            if step == 1 and half == 0:
                @pl.when(mine == 1)
                def _():
                    for array in range(2):
                        local_send(array).wait_recv()

            def run(tile, carry):
                if step < n - 1:
                    for extra in range(per_tile):
                        index = (half * tiles + tile) * per_tile + extra
                        for behind in (-step - 1, step + 1):
                            @pl.when((me + behind >= 0) & (me + behind < n))
                            def _():
                                forward(me + behind, index)
                queries = queries_of(doc, head, tile)
                if step == 0:
                    out, peak, total = prefix(queries, owner, head)
                    first[head, tile] = out
                    stat[head, tile, 0] = jnp.broadcast_to(peak, out.shape)
                    stat[head, tile, 1] = jnp.broadcast_to(total, out.shape)
                    return carry
                join(owner, head, tile, prefix(queries, owner, head), local(queries, doc, head))
                if step == 1:
                    queries = queries_of(doc_list[0], head, tile)
                    peak = stat[head, tile, 0][:, 0:1]
                    total = stat[head, tile, 1][:, 0:1]
                    join(owners[0], head, tile, (first[head, tile], peak, total), local(queries, doc_list[0], head))
                return carry

            lax.fori_loop(0, tiles, run, 0)
        for done in ([], owners[:2], owners[step:step + 1])[min(step, 2)]:
            pltpu.make_async_copy(held.at[done], out_hbm.at[done], out_sem.at[done]).start()

    own_sends(lambda copy: copy.wait_send())

    @pl.when(mine == 0)
    def _():
        for array in range(2):
            local_send(array).wait_send()

    for step in range(1, n):
        owner = owners[step]
        for place, listed in carried.items():
            @pl.when(mine == place)
            def _():
                for head, array, part in listed:
                    slot = array * kv + head
                    passed(owner, slot, part, "x").wait_send()

                    @pl.when(goes_on(owner))
                    def _():
                        passed(owner, slot, part, "z").wait_send()
    for owner in owners:
        pltpu.make_async_copy(held.at[owner], out_hbm.at[owner], out_sem.at[owner]).wait()


def reorder_kernel(tmpl, table, source, target, staged, in_sem, out_sem):
    docs = source.shape[0]
    loads = [
        pltpu.make_async_copy(source.at[table[tmpl[doc, 0]]], staged.at[doc], in_sem.at[doc]) for doc in range(docs)]
    stores = [pltpu.make_async_copy(staged.at[doc], target.at[doc], out_sem.at[doc]) for doc in range(docs)]
    for load in loads:
        load.start()
    for load, store in zip(loads, stores):
        load.wait()
        store.start()
    for store in stores:
        store.wait()


def shared(n, queries, doc_keys, doc_values, prefix_keys, prefix_values, template, owner_table):
    kv = KVH // lax.axis_size("tp")
    docs, span, feats = queries.shape
    length = prefix_keys.shape[1]
    groups = H // KVH
    tiles, tile_rows = groups // HEADS_TILE, HEADS_TILE * span
    slots = 2 * kv
    in_hbm = pl.BlockSpec(memory_space=pltpu.HBM)
    scalars = pl.BlockSpec(memory_space=pltpu.SMEM)
    dma = pltpu.SemaphoreType.DMA
    scores = docs * feats // HD * span * (length + 2 * span)
    by_owner = pl.pallas_call(
        functools.partial(shared_kernel, n, kv),
        out_shape=jax.ShapeDtypeStruct(queries.shape, queries.dtype),
        in_specs=[in_hbm] * 5 + [scalars] * 2,
        out_specs=in_hbm,
        scratch_shapes=[
            pltpu.VMEM(queries.shape, jnp.bfloat16),
            pltpu.VMEM((2,) + doc_keys.shape, jnp.bfloat16),
            pltpu.VMEM((2,) + doc_keys.shape, jnp.bfloat16),
            pltpu.VMEM((n, slots, length, HD), jnp.bfloat16),
            pltpu.VMEM(queries.shape, jnp.bfloat16),
            pltpu.VMEM((kv, tiles, tile_rows, HD), jnp.bfloat16),
            pltpu.VMEM((kv, tiles, 2, tile_rows, HD), jnp.float32),
            dma((3,)),
            dma((slots,)),
            dma((2,)),
            dma((2,)),
            dma((slots, ROW_CHUNKS)),
            dma((slots, ROW_CHUNKS)),
            dma((n, slots, ROW_CHUNKS)),
            dma((n, slots, ROW_CHUNKS)),
            dma((n, slots, ROW_CHUNKS)),
            dma((n,)),
        ],
        compiler_params=pltpu.CompilerParams(
            collective_id=0, has_side_effects=True, vmem_limit_bytes=62 * 2 ** 20),
        cost_estimate=pl.CostEstimate(
            flops=4 * HD * scores, bytes_accessed=8 * 2 ** 20, transcendentals=scores),
    )(queries, doc_keys, doc_values, prefix_keys, prefix_values, template, owner_table)
    return pl.pallas_call(
        reorder_kernel,
        out_shape=jax.ShapeDtypeStruct(queries.shape, queries.dtype),
        in_specs=[scalars] * 2 + [in_hbm],
        out_specs=in_hbm,
        scratch_shapes=[pltpu.VMEM(queries.shape, queries.dtype), dma((docs,)), dma((docs,))],
        compiler_params=pltpu.CompilerParams(vmem_limit_bytes=62 * 2 ** 20),
    )(template, owner_table, by_owner)


def route(queries, doc_keys, doc_values, prefix_keys, prefix_values, template, owner_table):
    n = lax.axis_size("pre")
    fits = (
        n == queries.shape[0] == owner_table.shape[0]
        and lax.axis_size("stg") == 2
        and KVH // lax.axis_size("tp") == 2
    )
    step = functools.partial(shared, n) if fits else shards
    return step(queries, doc_keys, doc_values, prefix_keys, prefix_values, template, owner_table)


def solution(mesh):
    return jax.shard_map(
        route,
        mesh=mesh,
        in_specs=(
            P(("grp", "pre"), "stg", "tp"),
            P(("grp", "pre"), "stg", "tp"),
            P(("grp", "pre"), "stg", "tp"),
            P(("grp", "pre"), None, "tp"),
            P(("grp", "pre"), None, "tp"),
            P(("grp", "pre"), None),
            P("grp"),
        ),
        out_specs=P(("grp", "pre"), "stg", "tp"),
        check_vma=False,
    )
```
